256 devices in a mesh: seq: 64 (over y, z_lo, x, core), head: 4 (over z_hi).
Axes of the slice: x: 4, y: 4, z: 8 (z_hi: 4, z_lo: 2; z = z_hi * 2 + z_lo), core: 2. Of those that a mesh axis runs over, the one named last changes fastest.
Arguments:
- query_keys: bfloat16 [32768, 4096], P('seq', 'head'), may hold values from -6 to 6
- values: bfloat16 [32768, 4096], P('seq', 'head'), may hold values from -7.5 to 7.5
- norm_gain: bfloat16 [4096], P('head'), may hold values from 0.25 to 1.75
- plan: int32 [2, 64], replicated, may hold values from 0 to 63, as said below
Outputs:
- normed: bfloat16 [32768, 4096], P('seq', 'head')
The draws below stay inside these ranges and needn't reach their ends.
Inputs may be any that keep to these rules, and one draw needn't show every extreme that they name: plan[r, b] = b XOR m_r, with 2 distinct nonzero round masks m_r; each round pairs every block with another block and no pair meets twice.
All inputs are finite; a program needn't handle non-finite values.
Results may differ from the reference program's by a relative error of at most 0.0055.
Values may be sent and summed in bfloat16 or wider, within the bound.
No kernel may reach another device: no remote copies, remote signals or barrier semaphores. Data moves between devices by JAX's collectives and lax.ppermute only.
A program may use at most 64 MiB of HBM per device.

```python
import math
import jax
import jax.numpy as jnp
from jax import lax

BLK = 512
HEADS = 32
HD = 128
ROUNDS = 2
NBLK = 64
TOKENS = 32768
WIDTH = 4096


def draw_query_keys(key, part):
    key = jax.random.fold_in(key, 2)
    first, second = jax.random.split(key, 2)
    base = jnp.clip(jax.random.normal(first, (TOKENS, WIDTH), jnp.float32), -4.0, 4.0)
    token_scale = jnp.exp(jax.random.uniform(second, (TOKENS, 1), jnp.float32, math.log(0.5), math.log(1.5)))
    result = base * token_scale
    return result.astype(jnp.bfloat16)


def draw_values(key, part):
    key = jax.random.fold_in(key, 3)
    first, second = jax.random.split(key, 2)
    head_index = (jnp.arange(WIDTH) // HD).astype(jnp.float32)
    base = jnp.clip(jax.random.normal(first, (TOKENS, WIDTH), jnp.float32), -4.0, 4.0)
    token_scale = jnp.exp(jax.random.uniform(second, (TOKENS, 1), jnp.float32, math.log(0.7), math.log(1.4)))
    exponent = 0.5
    rising = jnp.exp(exponent * math.log(3.0) * head_index / (HEADS - 1))
    return (0.7 * base * token_scale * rising[None, :]).astype(jnp.bfloat16)


def draw_plan(key, part):
    key = jax.random.fold_in(key, 1)
    order = jax.random.permutation(key, NBLK - 1) + 1
    round_masks = order[:ROUNDS].astype(jnp.int32)
    blocks = jnp.arange(NBLK, dtype=jnp.int32)
    return jnp.bitwise_xor(blocks[None, :], round_masks[:, None]).astype(jnp.int32)


def setup_inputs(seed: int = 0) -> dict:
    arg_keys = jax.random.split(jax.random.key(seed), 5)
    return {
        "query_keys": draw_query_keys(jax.random.fold_in(arg_keys[4], 71), 0),
        "values": draw_values(jax.random.fold_in(arg_keys[4], 71), 0),
        "norm_gain": jnp.clip(1.0 + 0.15 * jax.random.normal(arg_keys[2], (WIDTH,), jnp.float32), 0.25, 1.75).astype(jnp.bfloat16),
        "plan": draw_plan(jax.random.fold_in(arg_keys[4], 71), 0),
    }


def score_tile(query_rows, query_other, value_other, with_self):
    score_scale = HD ** (-0.5)
    scores = jnp.einsum('qhd,khd->hqk', query_rows.astype(jnp.float32), query_other.astype(jnp.float32)) * score_scale
    if with_self:
        diagonal_mask = jnp.eye(BLK, dtype=bool)
        scores = jnp.where(diagonal_mask[None], -jnp.inf, scores)
    peaks = lax.optimization_barrier(jnp.max(scores, axis=-1))
    expon = jnp.exp(scores - peaks[..., None])
    totals = lax.optimization_barrier(jnp.sum(expon, axis=-1))
    weights = lax.optimization_barrier(expon.astype(jnp.bfloat16)).astype(jnp.float32)
    partial_value = jnp.einsum('hqk,khd->qhd', weights, value_other.astype(jnp.float32)).astype(jnp.bfloat16)
    return (partial_value, peaks, totals)

def reference(query_keys, values, norm_gain, plan):
    query_blocks = query_keys.reshape(NBLK, BLK, HEADS, HD)
    value_blocks = values.reshape(NBLK, BLK, HEADS, HD)

    def one_block(block_id):
        query_rows = query_blocks[block_id]
        pieces = [score_tile(query_rows, query_rows, value_blocks[block_id], True)]
        for round_id in range(ROUNDS):
            partner = plan[round_id, block_id].astype(jnp.int32)
            pieces.append(score_tile(query_rows, query_blocks[partner], value_blocks[partner], False))
        overall = pieces[0][1]
        for piece in pieces[1:]:
            overall = jnp.maximum(overall, piece[1])
        weighted = jnp.zeros((BLK, HEADS, HD), jnp.float32)
        denominator = jnp.zeros((HEADS, BLK), jnp.float32)
        for partial_value, peaks, totals in pieces:
            factor = jnp.exp(peaks - overall)
            wide = lax.optimization_barrier(partial_value).astype(jnp.float32)
            weighted = weighted + factor.T[:, :, None] * wide
            denominator = denominator + factor * totals
        return weighted / denominator.T[:, :, None]
    attended = lax.map(one_block, jnp.arange(NBLK, dtype=jnp.int32)).reshape(TOKENS, WIDTH)
    power = lax.optimization_barrier(jnp.mean(attended * attended, axis=1, keepdims=True))
    return (attended * lax.rsqrt(power + 1e-06) * norm_gain.astype(jnp.float32)).astype(jnp.bfloat16)
```

```python
import functools

import jax
import jax.numpy as jnp
import numpy as np
from jax import lax
from jax.experimental import pallas as pl
from jax.experimental.pallas import tpu as pltpu
from jax.sharding import PartitionSpec as P

HD = 128
LANES = 128
EPS = 1e-6
SCALE = HD**-0.5 * float(np.log2(np.e))
VMEM_LIMIT = 40 * 1024 * 1024
CHUNK = 256


def planes_of(bits):
    found = []
    for v in range(1, 1 << bits):
        q = v.bit_length() - 1
        for u in range(1, 1 << bits):
            p = u.bit_length() - 1
            if p > q and not (u >> q) & 1:
                found.append((u, v, p, q))
    return found


def lookup(bits, planes):
    size = 1 << (bits + 1)
    entry = {}
    for number, (u, v, p, q) in enumerate(planes):
        for a in (u, v, u ^ v):
            for b in (u, v, u ^ v):
                if a != b:
                    entry[a, b] = number * 64 + (p + 1) * 8 + q + 1
    table = np.zeros(size * size, np.int32)
    for first in range(1, size):
        for second in range(1, size):
            if first != second:
                a, b = first >> 1, second >> 1
                if (a, b) not in entry:
                    a |= b
                    b = 4 if a != 4 else 1
                table[first * size + second] = entry[a, b]
    return table


def groups_of(size, u, v):
    span = [c ^ s ^ t for t in (0, v) for s in (0, u) for c in (0, 1)]
    seen, groups = set(), []
    for block in range(size):
        if block not in seen:
            base = block
            for mask in (u, v, 1):
                base = min(base, base ^ mask)
            coset = [base ^ mask for mask in span]
            seen |= set(coset)
            groups.append(coset)
    return groups


def swap_all(groups):
    def run(parts):
        return lax.all_to_all(parts, "seq", 0, 0, axis_index_groups=groups, tiled=True)

    return run


def pack_kernel(query_keys, values, out):
    for h in range(out.shape[0]):
        out[h, 0] = query_keys[:, h * HD : (h + 1) * HD]
        out[h, 1] = values[:, h * HD : (h + 1) * HD]


def attend_kernel(ids, blocks, out, ext):
    members, _, block_len, _ = blocks.shape
    for t in range(members):
        ext[t, :, :HD] = blocks[t, 1]
        ext[t, :, HD:] = jnp.ones((block_len, LANES), jnp.bfloat16)
    row_ids = lax.broadcasted_iota(jnp.int32, (CHUNK, CHUNK), 0)
    col_ids = lax.broadcasted_iota(jnp.int32, (CHUNK, CHUNK), 1)
    diagonal = row_ids == col_ids

    def unit(t, _):
        others = (t, t ^ ids[0], t ^ ids[1])
        for start in range(0, block_len, CHUNK):
            rows = blocks[t, 0, start : start + CHUNK, :]
            scores = [
                lax.dot_general(
                    rows, blocks[other, 0], (((1,), (1,)), ((), ())), preferred_element_type=jnp.float32
                )
                for other in others
            ]
            pieces = [scores[0][:, c : c + CHUNK] for c in range(0, block_len, CHUNK)]
            pieces[start // CHUNK] = jnp.where(diagonal, -jnp.inf, pieces[start // CHUNK])
            scores[0] = jnp.concatenate(pieces, axis=1)
            peak = functools.reduce(jnp.maximum, scores)
            peak = jnp.max(peak, axis=1, keepdims=True) * SCALE
            total = None
            for score, other in zip(scores, others, strict=True):
                weight = jnp.exp2(score * SCALE - peak).astype(jnp.bfloat16)
                part = jnp.dot(weight, ext[other], preferred_element_type=jnp.float32)
                total = part if total is None else total + part
            out[t, start : start + CHUNK, :] = (total[:, :HD] / total[:, HD:]).astype(jnp.bfloat16)
        return 0

    lax.fori_loop(0, members, unit, 0)


def square_kernel(attended, out):
    ones = jnp.ones((8, HD), jnp.bfloat16)
    total = None
    for h in range(attended.shape[0]):
        wide = attended[h].astype(jnp.float32)
        square = wide * wide
        high = square.astype(jnp.bfloat16)
        low = (square - high.astype(jnp.float32)).astype(jnp.bfloat16)
        for part in (high, low):
            term = lax.dot_general(ones, part, (((1,), (1,)), ((), ())), preferred_element_type=jnp.float32)
            total = term if total is None else total + term
    for copy in range(out.shape[0]):
        out[copy] = total


def norm_kernel(sums, attended, gain, out, *, features):
    power = functools.reduce(jnp.add, [sums[i] for i in range(sums.shape[0])]) / features
    factor = jnp.transpose(lax.rsqrt(power + EPS))[:, :1]
    for h in range(attended.shape[0]):
        columns = slice(h * HD, (h + 1) * HD)
        scaled = attended[h].astype(jnp.float32) * factor * gain[:, columns].astype(jnp.float32)
        out[:, columns] = scaled.astype(jnp.bfloat16)


def call(kernel, shape, dtype, *args, scalars=(), scratch=()):
    vmem = pl.BlockSpec(memory_space=pltpu.VMEM)
    smem = pl.BlockSpec(memory_space=pltpu.SMEM)
    return pl.pallas_call(
        kernel,
        out_shape=jax.ShapeDtypeStruct(shape, dtype),
        in_specs=[smem] * len(scalars) + [vmem] * len(args),
        out_specs=vmem,
        scratch_shapes=list(scratch),
        compiler_params=pltpu.CompilerParams(vmem_limit_bytes=VMEM_LIMIT),
    )(*scalars, *args)


def local(query_keys, values, norm_gain, plan):
    size = lax.axis_size("seq")
    head_size = lax.axis_size("head")
    block_len, local_width = query_keys.shape
    heads = local_width // HD

    planes = planes_of(size.bit_length() - 2)
    first, second = plan[0, 0], plan[1, 0]
    entry = jnp.asarray(lookup(size.bit_length() - 2, planes))[first * size + second]
    plane, p, q = entry // 64, (entry // 8) % 8, entry % 8

    def place(mask):
        return (mask & 1) | (((mask >> p) & 1) << 1) | (((mask >> q) & 1) << 2)

    ids = jnp.stack([place(first), place(second)]).astype(jnp.int32)
    routes = [swap_all(groups_of(size, 2 * u, 2 * v)) for u, v, _, _ in planes]

    packed = call(pack_kernel, (heads, 2, block_len, HD), jnp.bfloat16, query_keys, values)
    blocks = lax.switch(plane, routes, packed)
    attended = call(
        attend_kernel,
        (heads, block_len, HD),
        jnp.bfloat16,
        blocks,
        scalars=(ids,),
        scratch=(pltpu.VMEM((heads, block_len, HD + LANES), jnp.bfloat16),),
    )
    mine = lax.switch(plane, routes, attended)
    squares = call(square_kernel, (head_size, 8, block_len), jnp.float32, mine)
    sums = lax.all_to_all(squares, "head", 0, 0, tiled=True)
    return call(
        functools.partial(norm_kernel, features=local_width * head_size),
        (block_len, local_width),
        jnp.bfloat16,
        sums,
        mine,
        norm_gain.reshape(1, local_width),
    )


def solution(mesh):
    in_specs = (P("seq", "head"), P("seq", "head"), P("head"), P())
    return jax.shard_map(local, mesh=mesh, in_specs=in_specs, out_specs=P("seq", "head"), check_vma=False)
```

```python
import functools

import jax
import jax.numpy as jnp
import numpy as np
from jax import lax
from jax.experimental import pallas as pl
from jax.experimental.pallas import tpu as pltpu
from jax.sharding import PartitionSpec as P

HD = 128
LANES = 128
EPS = 1e-6
SCALE = HD**-0.5 * float(np.log2(np.e))
VMEM_LIMIT = 40 * 1024 * 1024
CHUNK = 256


def planes_of(bits):
    found = []
    for v in range(1, 1 << bits):
        q = v.bit_length() - 1
        for u in range(1, 1 << bits):
            p = u.bit_length() - 1
            if p > q and not (u >> q) & 1:
                found.append((u, v, p, q))
    return found


def lookup(bits, planes):
    size = 1 << bits
    entry = {}
    for number, (u, v, p, q) in enumerate(planes):
        for a in (u, v, u ^ v):
            for b in (u, v, u ^ v):
                if a != b:
                    entry[a, b] = (number + 1) << 6 | (p + 1) << 3 | q + 1
    table = np.zeros((size, size), np.int32)
    for first in range(size):
        for second in range(size):
            a, b = first, second
            if a | b:
                if (a, b) not in entry:
                    a |= b
                    b = 4 if a != 4 else 1
                table[first, second] = entry[a, b]
    return table


def groups_of(size, u, v):
    span = [c ^ s ^ t for t in (0, v) for s in (0, u) for c in (0, 1)]
    seen, groups = set(), []
    for block in range(size):
        if block not in seen:
            base = block
            for mask in (u, v, 1):
                base = min(base, base ^ mask)
            coset = [base ^ mask for mask in span]
            seen |= set(coset)
            groups.append(coset)
    return groups


def swap_all(groups):
    def run(parts):
        return lax.all_to_all(parts, "seq", 0, 0, axis_index_groups=groups, tiled=True)

    return run


def over_head(values, bit_mask):
    return lax.ppermute(values, "head", [(i, i ^ bit_mask) for i in range(lax.axis_size("head"))])


def head_swaps(parts):
    return over_head(over_head(parts, 1), 3)


def route_kernel(plan, table, plane, ids):
    first, second = plan[0, 0], plan[1, 0]
    entry = table[first >> 1, second >> 1]
    p, q = (entry >> 3) & 7, entry & 7
    plane[0] = entry >> 6
    for i, mask in enumerate((first, second)):
        ids[i] = (mask & 1) | (((mask >> p) & 1) << 1) | (((mask >> q) & 1) << 2)


def pack_kernel(query_keys, values, out):
    for h in range(out.shape[0]):
        out[h, 0] = query_keys[:, h * HD : (h + 1) * HD]
        out[h, 1] = values[:, h * HD : (h + 1) * HD]


def attend_kernel(ids, blocks, out, ext):
    members, _, block_len, _ = blocks.shape
    for t in range(members):
        ext[t, :, :HD] = blocks[t, 1]
        ext[t, :, HD:] = jnp.ones((block_len, LANES), jnp.bfloat16)
    row_ids = lax.broadcasted_iota(jnp.int32, (CHUNK, CHUNK), 0)
    col_ids = lax.broadcasted_iota(jnp.int32, (CHUNK, CHUNK), 1)
    diagonal = row_ids == col_ids

    def unit(t, _):
        others = (t, t ^ ids[0], t ^ ids[1])

        def scores_of(start):
            rows = blocks[t, 0, start : start + CHUNK, :]
            scores = [
                lax.dot_general(
                    rows, blocks[other, 0], (((1,), (1,)), ((), ())), preferred_element_type=jnp.float32
                )
                for other in others
            ]
            pieces = [scores[0][:, c : c + CHUNK] for c in range(0, block_len, CHUNK)]
            pieces[start // CHUNK] = jnp.where(diagonal, -jnp.inf, pieces[start // CHUNK])
            scores[0] = jnp.concatenate(pieces, axis=1)
            return scores

        def finish(start, scores):
            peak = functools.reduce(jnp.maximum, scores)
            peak = jnp.max(peak, axis=1, keepdims=True) * SCALE
            total = None
            for score, other in zip(scores, others, strict=True):
                weight = jnp.exp2(score * SCALE - peak).astype(jnp.bfloat16)
                part = jnp.dot(weight, ext[other], preferred_element_type=jnp.float32)
                total = part if total is None else total + part
            out[t, start : start + CHUNK, :] = (total[:, :HD] / total[:, HD:]).astype(jnp.bfloat16)

        scores = scores_of(0)
        for start in range(0, block_len, CHUNK):
            later = scores_of(start + CHUNK) if start + CHUNK < block_len else None
            finish(start, scores)
            scores = later
        return 0

    lax.fori_loop(0, members, unit, 0, unroll=2)


def square_kernel(attended, out):
    ones = jnp.ones((8, HD), jnp.bfloat16)
    total = None
    for h in range(attended.shape[0]):
        wide = attended[h].astype(jnp.float32)
        square = wide * wide
        high = square.astype(jnp.bfloat16)
        low = (square - high.astype(jnp.float32)).astype(jnp.bfloat16)
        for part in (high, low):
            term = lax.dot_general(ones, part, (((1,), (1,)), ((), ())), preferred_element_type=jnp.float32)
            total = term if total is None else total + term
    out[...] = total


def norm_kernel(near, far, attended, gain, out, *, features):
    power = (near[...] + far[...]) / features
    factor = jnp.transpose(lax.rsqrt(power + EPS))[:, :1]
    for h in range(attended.shape[0]):
        columns = slice(h * HD, (h + 1) * HD)
        scaled = attended[h].astype(jnp.float32) * factor * gain[:, columns].astype(jnp.float32)
        out[:, columns] = scaled.astype(jnp.bfloat16)


def call(kernel, shape, dtype, *args, scalars=(), scratch=()):
    vmem = pl.BlockSpec(memory_space=pltpu.VMEM)
    smem = pl.BlockSpec(memory_space=pltpu.SMEM)
    return pl.pallas_call(
        kernel,
        out_shape=jax.ShapeDtypeStruct(shape, dtype),
        in_specs=[smem] * len(scalars) + [vmem] * len(args),
        out_specs=vmem,
        scratch_shapes=list(scratch),
        compiler_params=pltpu.CompilerParams(vmem_limit_bytes=VMEM_LIMIT),
    )(*scalars, *args)


def local(query_keys, values, norm_gain, plan):
    size = lax.axis_size("seq")
    head_size = lax.axis_size("head")
    block_len, local_width = query_keys.shape
    heads = local_width // HD

    chip_bits = size.bit_length() - 2
    planes = planes_of(chip_bits)
    swaps = [swap_all(groups_of(size, 2 * u, 2 * v)) for u, v, _, _ in planes]
    smem = pl.BlockSpec(memory_space=pltpu.SMEM)
    plane, ids = pl.pallas_call(
        route_kernel,
        out_shape=(jax.ShapeDtypeStruct((1,), jnp.int32), jax.ShapeDtypeStruct((2,), jnp.int32)),
        in_specs=[smem, smem],
        out_specs=(smem, smem),
    )(plan, jnp.asarray(lookup(chip_bits, planes)))
    plane = plane.reshape(())

    packed = call(pack_kernel, (heads, 2, block_len, HD), jnp.bfloat16, query_keys, values)
    blocks = lax.switch(plane, [head_swaps, *swaps], packed)
    attended = call(
        attend_kernel,
        (heads, block_len, HD),
        jnp.bfloat16,
        blocks,
        scalars=(ids,),
        scratch=(pltpu.VMEM((heads, block_len, HD + LANES), jnp.bfloat16),),
    )
    mine = lax.switch(plane, [head_swaps, *swaps], attended)
    squares = call(square_kernel, (8, block_len), jnp.float32, mine)
    near = squares + over_head(squares, 1)
    far = over_head(near, 3)
    return call(
        functools.partial(norm_kernel, features=local_width * head_size),
        (block_len, local_width),
        jnp.bfloat16,
        near,
        far,
        mine,
        norm_gain.reshape(1, local_width),
    )


def solution(mesh):
    in_specs = (P("seq", "head"), P("seq", "head"), P("head"), P())
    return jax.shard_map(local, mesh=mesh, in_specs=in_specs, out_specs=P("seq", "head"), check_vma=False)
```

```python
import functools

import jax
import jax.numpy as jnp
import numpy as np
from jax import lax
from jax.experimental import pallas as pl
from jax.experimental.pallas import tpu as pltpu
from jax.sharding import PartitionSpec as P

HD = 128
LANES = 128
EPS = 1e-6
SCALE = HD**-0.5 * float(np.log2(np.e))
VMEM_LIMIT = 40 * 1024 * 1024
CHUNK = 256
FANOUT = (6, 1)


def planes_of(bits):
    found = []
    for v in range(1, 1 << bits):
        q = v.bit_length() - 1
        for u in range(1, 1 << bits):
            p = u.bit_length() - 1
            if p > q and not (u >> q) & 1:
                found.append((u, v, p, q))
    return found


def lookup(bits, planes):
    size = 1 << bits
    entry = {}
    for number, (u, v, p, q) in enumerate(planes):
        for a in (u, v, u ^ v):
            for b in (u, v, u ^ v):
                if a != b:
                    route = (1 + number // FANOUT[0], number % FANOUT[0] // FANOUT[1], number % FANOUT[1])
                    entry[a, b] = route[0] << 22 | route[1] << 14 | route[2] << 6 | (p + 1) << 3 | q + 1
    table = np.zeros((size, size), np.int32)
    for first in range(size):
        for second in range(size):
            a, b = first, second
            if a | b:
                if (a, b) not in entry:
                    a |= b
                    b = 4 if a != 4 else 1
                table[first, second] = entry[a, b]
    return table


def groups_of(size, u, v):
    span = [c ^ s ^ t for t in (0, v) for s in (0, u) for c in (0, 1)]
    seen, groups = set(), []
    for block in range(size):
        if block not in seen:
            base = block
            for mask in (u, v, 1):
                base = min(base, base ^ mask)
            coset = [base ^ mask for mask in span]
            seen |= set(coset)
            groups.append(coset)
    return groups


def swap_all(groups):
    def run(parts):
        return lax.all_to_all(parts, "seq", 0, 0, axis_index_groups=groups, tiled=True)

    return run


def over_head(values, bit_mask):
    return lax.ppermute(values, "head", [(i, i ^ bit_mask) for i in range(lax.axis_size("head"))])


def head_swaps(parts):
    for _ in range(2):
        parts = over_head(over_head(parts, 1), 3)
    return parts


def routed(route, swaps, parts, first):
    def level(planes, depth):
        if len(planes) == 1:
            return planes[0]
        size = (*FANOUT, 1)[depth]
        branches = [level(planes[i : i + size], depth + 1) for i in range(0, len(planes), size)]
        if len(branches) == 1:
            return branches[0]
        return lambda data: lax.switch(route[depth], branches, data)

    outer = [level(swaps[i : i + FANOUT[0]], 1) for i in range(0, len(swaps), FANOUT[0])]
    return lax.switch(route[0], [first, *outer], parts)


def route_kernel(plan, table, outer, middle, inner, ids):
    first, second = plan[0, 0], plan[1, 0]
    entry = table[first >> 1, second >> 1]
    p, q = (entry >> 3) & 7, entry & 7
    outer[0] = entry >> 22
    middle[0] = (entry >> 14) & 255
    inner[0] = (entry >> 6) & 255
    for i, mask in enumerate((first, second)):
        ids[i] = (mask & 1) | (((mask >> p) & 1) << 1) | (((mask >> q) & 1) << 2)


def pack_kernel(query_keys, values, out):
    for h in range(out.shape[0]):
        out[h, 0] = query_keys[:, h * HD : (h + 1) * HD]
        out[h, 1] = values[:, h * HD : (h + 1) * HD]


def attend_kernel(ids, blocks, out, ext):
    members, _, block_len, _ = blocks.shape
    for t in range(members):
        ext[t, :, :HD] = blocks[t, 1]
        ext[t, :, HD:] = jnp.ones((block_len, LANES), jnp.bfloat16)
    row_ids = lax.broadcasted_iota(jnp.int32, (CHUNK, CHUNK), 0)
    col_ids = lax.broadcasted_iota(jnp.int32, (CHUNK, CHUNK), 1)
    diagonal = row_ids == col_ids

    def unit(t, _):
        others = (t, t ^ ids[0], t ^ ids[1])

        def scores_of(start):
            rows = blocks[t, 0, start : start + CHUNK, :]
            scores = [
                lax.dot_general(
                    rows, blocks[other, 0], (((1,), (1,)), ((), ())), preferred_element_type=jnp.float32
                )
                for other in others
            ]
            pieces = [scores[0][:, c : c + CHUNK] for c in range(0, block_len, CHUNK)]
            pieces[start // CHUNK] = jnp.where(diagonal, -jnp.inf, pieces[start // CHUNK])
            scores[0] = jnp.concatenate(pieces, axis=1)
            return scores

        def finish(start, scores):
            peak = functools.reduce(jnp.maximum, scores)
            peak = jnp.max(peak, axis=1, keepdims=True) * SCALE
            total = None
            for score, other in zip(scores, others, strict=True):
                weight = jnp.exp2(score * SCALE - peak).astype(jnp.bfloat16)
                part = jnp.dot(weight, ext[other], preferred_element_type=jnp.float32)
                total = part if total is None else total + part
            out[t, start : start + CHUNK, :] = (total[:, :HD] / total[:, HD:]).astype(jnp.bfloat16)

        scores = scores_of(0)
        for start in range(0, block_len, CHUNK):
            later = scores_of(start + CHUNK) if start + CHUNK < block_len else None
            finish(start, scores)
            scores = later
        return 0

    lax.fori_loop(0, members, unit, 0, unroll=1)


def square_kernel(attended, out):
    ones = jnp.ones((8, HD), jnp.bfloat16)
    total = None
    for h in range(attended.shape[0]):
        wide = attended[h].astype(jnp.float32)
        square = wide * wide
        high = square.astype(jnp.bfloat16)
        low = (square - high.astype(jnp.float32)).astype(jnp.bfloat16)
        for part in (high, low):
            term = lax.dot_general(ones, part, (((1,), (1,)), ((), ())), preferred_element_type=jnp.float32)
            total = term if total is None else total + term
    out[...] = total


def norm_kernel(near, far, attended, gain, out, *, features):
    power = (near[...] + far[...]) / features
    factor = jnp.transpose(lax.rsqrt(power + EPS))[:, :1]
    for h in range(attended.shape[0]):
        columns = slice(h * HD, (h + 1) * HD)
        scaled = attended[h].astype(jnp.float32) * factor * gain[:, columns].astype(jnp.float32)
        out[:, columns] = scaled.astype(jnp.bfloat16)


def call(kernel, shape, dtype, *args, scalars=(), scratch=()):
    vmem = pl.BlockSpec(memory_space=pltpu.VMEM)
    smem = pl.BlockSpec(memory_space=pltpu.SMEM)
    return pl.pallas_call(
        kernel,
        out_shape=jax.ShapeDtypeStruct(shape, dtype),
        in_specs=[smem] * len(scalars) + [vmem] * len(args),
        out_specs=vmem,
        scratch_shapes=list(scratch),
        compiler_params=pltpu.CompilerParams(vmem_limit_bytes=VMEM_LIMIT),
    )(*scalars, *args)


def local(query_keys, values, norm_gain, plan):
    size = lax.axis_size("seq")
    head_size = lax.axis_size("head")
    block_len, local_width = query_keys.shape
    heads = local_width // HD

    chip_bits = size.bit_length() - 2
    planes = planes_of(chip_bits)
    swaps = [swap_all(groups_of(size, 2 * u, 2 * v)) for u, v, _, _ in planes]
    smem = pl.BlockSpec(memory_space=pltpu.SMEM)
    *route, ids = pl.pallas_call(
        route_kernel,
        out_shape=[jax.ShapeDtypeStruct((n,), jnp.int32) for n in (1, 1, 1, 2)],
        in_specs=[smem, smem],
        out_specs=[smem] * 4,
    )(plan, jnp.asarray(lookup(chip_bits, planes)))
    route = [number.reshape(()) for number in route]

    packed = call(pack_kernel, (heads, 2, block_len, HD), jnp.bfloat16, query_keys, values)
    blocks = routed(route, swaps, packed, head_swaps)
    attended = call(
        attend_kernel,
        (heads, block_len, HD),
        jnp.bfloat16,
        blocks,
        scalars=(ids,),
        scratch=(pltpu.VMEM((heads, block_len, HD + LANES), jnp.bfloat16),),
    )
    mine = routed(route, swaps, attended, lambda parts: parts)
    squares = call(square_kernel, (8, block_len), jnp.float32, mine)
    near = squares + over_head(squares, 1)
    far = over_head(near, 3)
    return call(
        functools.partial(norm_kernel, features=local_width * head_size),
        (block_len, local_width),
        jnp.bfloat16,
        near,
        far,
        mine,
        norm_gain.reshape(1, local_width),
    )


def solution(mesh):
    in_specs = (P("seq", "head"), P("seq", "head"), P("head"), P())
    return jax.shard_map(local, mesh=mesh, in_specs=in_specs, out_specs=P("seq", "head"), check_vma=False)
```

```python
import functools

import jax
import jax.numpy as jnp
import numpy as np
from jax import lax
from jax.experimental import pallas as pl
from jax.experimental.pallas import tpu as pltpu
from jax.sharding import PartitionSpec as P

HD = 128
LANES = 128
EPS = 1e-6
SCALE = HD**-0.5 * float(np.log2(np.e))
VMEM_LIMIT = 40 * 1024 * 1024
CHUNK = 256


def planes_of(bits):
    found = []
    for v in range(1, 1 << bits):
        q = v.bit_length() - 1
        for u in range(1, 1 << bits):
            p = u.bit_length() - 1
            if p > q and not (u >> q) & 1:
                found.append((u, v, p, q))
    return found


def lookup(bits, planes):
    size = 1 << bits
    entry = {}
    for number, (u, v, p, q) in enumerate(planes):
        for a in (u, v, u ^ v):
            for b in (u, v, u ^ v):
                if a != b:
                    entry[a, b] = (number + 1) << 6 | (p + 1) << 3 | q + 1
    table = np.zeros((size, size), np.int32)
    for first in range(size):
        for second in range(size):
            a, b = first, second
            if a | b:
                if (a, b) not in entry:
                    a |= b
                    b = 4 if a != 4 else 1
                table[first, second] = entry[a, b]
    return table


def groups_of(size, u, v):
    span = [c ^ s ^ t for t in (0, v) for s in (0, u) for c in (0, 1)]
    seen, groups = set(), []
    for block in range(size):
        if block not in seen:
            base = block
            for mask in (u, v, 1):
                base = min(base, base ^ mask)
            coset = [base ^ mask for mask in span]
            seen |= set(coset)
            groups.append(coset)
    return groups


def swap_all(groups):
    def run(parts):
        return lax.all_to_all(parts, "seq", 0, 0, axis_index_groups=groups, tiled=True)

    return run


def over_head(values, bit_mask):
    return lax.ppermute(values, "head", [(i, i ^ bit_mask) for i in range(lax.axis_size("head"))])


def head_swaps(parts):
    return over_head(over_head(parts, 1), 3)


def route_kernel(plan, table, plane, ids):
    first, second = plan[0, 0], plan[1, 0]
    entry = table[first >> 1, second >> 1]
    p, q = (entry >> 3) & 7, entry & 7
    plane[0] = entry >> 6
    for i, mask in enumerate((first, second)):
        ids[i] = (mask & 1) | (((mask >> p) & 1) << 1) | (((mask >> q) & 1) << 2)


def pack_kernel(query_keys, values, out):
    for h in range(out.shape[0]):
        out[h, 0] = query_keys[:, h * HD : (h + 1) * HD]
        out[h, 1] = values[:, h * HD : (h + 1) * HD]


def step_kernel(step, ids, arrived, out, squares, ext):
    pl.when(step[0] == 0)(lambda: attend(ids, arrived, out, ext))
    pl.when(step[0] != 0)(lambda: gather(arrived, out, squares))


def gather(arrived, out, squares):
    ones = jnp.ones((8, HD), jnp.bfloat16)
    total = None
    for h in range(arrived.shape[0]):
        attended = arrived[h, 0]
        out[h, 0] = attended
        wide = attended.astype(jnp.float32)
        square = wide * wide
        high = square.astype(jnp.bfloat16)
        low = (square - high.astype(jnp.float32)).astype(jnp.bfloat16)
        for part in (high, low):
            term = lax.dot_general(ones, part, (((1,), (1,)), ((), ())), preferred_element_type=jnp.float32)
            total = term if total is None else total + term
    squares[...] = total


def attend(ids, blocks, out, ext):
    members, _, block_len, _ = blocks.shape
    for t in range(members):
        ext[t, :, :HD] = blocks[t, 1]
        ext[t, :, HD:] = jnp.ones((block_len, LANES), jnp.bfloat16)
    row_ids = lax.broadcasted_iota(jnp.int32, (CHUNK, CHUNK), 0)
    col_ids = lax.broadcasted_iota(jnp.int32, (CHUNK, CHUNK), 1)
    diagonal = row_ids == col_ids

    def unit(t, _):
        others = (t, t ^ ids[0], t ^ ids[1])

        def scores_of(start):
            rows = blocks[t, 0, start : start + CHUNK, :]
            scores = [
                lax.dot_general(
                    rows, blocks[other, 0], (((1,), (1,)), ((), ())), preferred_element_type=jnp.float32
                )
                for other in others
            ]
            pieces = [scores[0][:, c : c + CHUNK] for c in range(0, block_len, CHUNK)]
            pieces[start // CHUNK] = jnp.where(diagonal, -jnp.inf, pieces[start // CHUNK])
            scores[0] = jnp.concatenate(pieces, axis=1)
            return scores

        def finish(start, scores):
            peak = functools.reduce(jnp.maximum, scores)
            peak = jnp.max(peak, axis=1, keepdims=True) * SCALE
            total = None
            for score, other in zip(scores, others, strict=True):
                weight = jnp.exp2(score * SCALE - peak).astype(jnp.bfloat16)
                part = jnp.dot(weight, ext[other], preferred_element_type=jnp.float32)
                total = part if total is None else total + part
            out[t, 0, start : start + CHUNK, :] = (total[:, :HD] / total[:, HD:]).astype(jnp.bfloat16)

        scores = scores_of(0)
        for start in range(0, block_len, CHUNK):
            later = scores_of(start + CHUNK) if start + CHUNK < block_len else None
            finish(start, scores)
            scores = later
        return 0

    lax.fori_loop(0, members, unit, 0, unroll=2)


def norm_kernel(near, far, attended, gain, out, *, features):
    power = (near[...] + far[...]) / features
    factor = jnp.transpose(lax.rsqrt(power + EPS))[:, :1]
    for h in range(attended.shape[0]):
        columns = slice(h * HD, (h + 1) * HD)
        scaled = attended[h, 0].astype(jnp.float32) * factor * gain[:, columns].astype(jnp.float32)
        out[:, columns] = scaled.astype(jnp.bfloat16)


def call(kernel, shape, dtype, *args, scalars=(), scratch=()):
    vmem = pl.BlockSpec(memory_space=pltpu.VMEM)
    smem = pl.BlockSpec(memory_space=pltpu.SMEM)
    return pl.pallas_call(
        kernel,
        out_shape=jax.ShapeDtypeStruct(shape, dtype),
        in_specs=[smem] * len(scalars) + [vmem] * len(args),
        out_specs=vmem,
        scratch_shapes=list(scratch),
        compiler_params=pltpu.CompilerParams(vmem_limit_bytes=VMEM_LIMIT),
    )(*scalars, *args)


def local(query_keys, values, norm_gain, plan):
    size = lax.axis_size("seq")
    head_size = lax.axis_size("head")
    block_len, local_width = query_keys.shape
    heads = local_width // HD

    chip_bits = size.bit_length() - 2
    planes = planes_of(chip_bits)
    swaps = [swap_all(groups_of(size, 2 * u, 2 * v)) for u, v, _, _ in planes]
    smem = pl.BlockSpec(memory_space=pltpu.SMEM)
    plane, ids = pl.pallas_call(
        route_kernel,
        out_shape=(jax.ShapeDtypeStruct((1,), jnp.int32), jax.ShapeDtypeStruct((2,), jnp.int32)),
        in_specs=[smem, smem],
        out_specs=(smem, smem),
    )(plan, jnp.asarray(lookup(chip_bits, planes)))
    plane = plane.reshape(())

    packed = call(pack_kernel, (heads, 2, block_len, HD), jnp.bfloat16, query_keys, values)
    routes = [head_swaps, *swaps]

    def body(step, carry):
        vmem = pl.BlockSpec(memory_space=pltpu.VMEM)
        return tuple(
            pl.pallas_call(
                step_kernel,
                out_shape=[
                    jax.ShapeDtypeStruct(packed.shape, jnp.bfloat16),
                    jax.ShapeDtypeStruct((8, block_len), jnp.float32),
                ],
                in_specs=[smem, smem, vmem],
                out_specs=[vmem, vmem],
                scratch_shapes=[pltpu.VMEM((heads, block_len, HD + LANES), jnp.bfloat16)],
                compiler_params=pltpu.CompilerParams(vmem_limit_bytes=VMEM_LIMIT),
            )(step.reshape(1), ids, lax.switch(plane, routes, carry[0]))
        )

    mine, squares = lax.fori_loop(0, 2, body, (packed, jnp.zeros((8, block_len), jnp.float32)))
    near = squares + over_head(squares, 1)
    far = over_head(near, 3)
    return call(
        functools.partial(norm_kernel, features=local_width * head_size),
        (block_len, local_width),
        jnp.bfloat16,
        near,
        far,
        mine,
        norm_gain.reshape(1, local_width),
    )


def solution(mesh):
    in_specs = (P("seq", "head"), P("seq", "head"), P("head"), P())
    return jax.shard_map(local, mesh=mesh, in_specs=in_specs, out_specs=P("seq", "head"), check_vma=False)
```

```python
import functools

import jax
import jax.numpy as jnp
import numpy as np
from jax import lax
from jax.experimental import pallas as pl
from jax.experimental.pallas import tpu as pltpu
from jax.sharding import PartitionSpec as P

HD = 128
LANES = 128
EPS = 1e-6
SCALE = HD**-0.5 * float(np.log2(np.e))
VMEM_LIMIT = 40 * 1024 * 1024
PACK_VMEM_LIMIT = 61 * 1024 * 1024
CHUNK = 256


def planes_of(bits):
    found = []
    for v in range(1, 1 << bits):
        q = v.bit_length() - 1
        for u in range(1, 1 << bits):
            p = u.bit_length() - 1
            if p > q and not (u >> q) & 1:
                found.append((u, v, p, q))
    return found


def lookup(bits, planes):
    size = 1 << bits
    entry = {}
    for number, (u, v, p, q) in enumerate(planes):
        for a in (u, v, u ^ v):
            for b in (u, v, u ^ v):
                if a != b:
                    entry[a, b] = (number + 1) << 6 | (p + 1) << 3 | q + 1
    table = np.zeros((size, size), np.int32)
    for first in range(size):
        for second in range(size):
            a, b = first, second
            if a | b:
                if (a, b) not in entry:
                    a |= b
                    b = 1 if a != 1 else 2
                table[first, second] = entry[a, b]
    return table


def groups_of(size, u, v):
    span = [c ^ s ^ t for t in (0, v) for s in (0, u) for c in (0, 1)]
    seen, groups = set(), []
    for block in range(size):
        if block not in seen:
            base = block
            for mask in (u, v, 1):
                base = min(base, base ^ mask)
            coset = [base ^ mask for mask in span]
            seen |= set(coset)
            groups.append(coset)
    return groups


def swap_all(groups):
    def run(parts):
        return lax.all_to_all(parts, "seq", 0, 0, axis_index_groups=groups, tiled=True)

    return run


def over_head(values, bit_mask):
    return lax.ppermute(values, "head", [(i, i ^ bit_mask) for i in range(lax.axis_size("head"))])


def head_swaps(parts):
    return over_head(over_head(parts, 1), 3)


def pack_kernel(plan_in, table_in, query_keys, values, out, plane, ids, plan, table, sems, scalar_sems):
    scalars = [
        pltpu.make_async_copy(plan_in, plan, scalar_sems.at[0]),
        pltpu.make_async_copy(table_in, table, scalar_sems.at[1]),
    ]
    for copy in scalars:
        copy.start()
    copies = []
    for part, array in enumerate((query_keys, values)):
        for h in range(out.shape[0]):
            columns = array.at[:, h * HD : (h + 1) * HD]
            copies.append(pltpu.make_async_copy(columns, out.at[h, part], sems.at[part, h]))
    for copy in copies:
        copy.start()
    for copy in scalars:
        copy.wait()
    first, second = plan[0, 0], plan[1, 0]
    entry = table[first >> 1, second >> 1]
    p, q = (entry >> 3) & 7, entry & 7
    plane[0] = entry >> 6
    for i, mask in enumerate((first, second)):
        ids[i] = (mask & 1) | (((mask >> p) & 1) << 1) | (((mask >> q) & 1) << 2)
    for copy in copies:
        copy.wait()


def step_kernel(step, ids, arrived, out, ext):
    pl.when(step[0] == 0)(lambda: attend(ids, arrived, out, ext))

    @pl.when(step[0] != 0)
    def _():
        for h in range(arrived.shape[0]):
            out[h, 0] = arrived[h, 0]


def attend(ids, blocks, out, ext):
    members, _, block_len, _ = blocks.shape
    for t in range(members):
        ext[t, :, :HD] = blocks[t, 1]
        ext[t, :, HD:] = jnp.ones((block_len, LANES), jnp.bfloat16)
    row_ids = lax.broadcasted_iota(jnp.int32, (CHUNK, CHUNK), 0)
    col_ids = lax.broadcasted_iota(jnp.int32, (CHUNK, CHUNK), 1)
    diagonal = row_ids == col_ids

    def unit(t, _):
        others = (t, t ^ ids[0], t ^ ids[1])

        def scores_of(start):
            rows = blocks[t, 0, start : start + CHUNK, :]
            scores = [
                lax.dot_general(
                    rows, blocks[other, 0], (((1,), (1,)), ((), ())), preferred_element_type=jnp.float32
                )
                for other in others
            ]
            pieces = [scores[0][:, c : c + CHUNK] for c in range(0, block_len, CHUNK)]
            pieces[start // CHUNK] = jnp.where(diagonal, -jnp.inf, pieces[start // CHUNK])
            scores[0] = jnp.concatenate(pieces, axis=1)
            return scores

        def finish(start, scores):
            peak = functools.reduce(jnp.maximum, scores)
            peak = jnp.max(peak, axis=1, keepdims=True) * SCALE
            total = None
            for score, other in zip(scores, others, strict=True):
                weight = jnp.exp2(score * SCALE - peak).astype(jnp.bfloat16)
                part = jnp.dot(weight, ext[other], preferred_element_type=jnp.float32)
                total = part if total is None else total + part
            out[t, 0, start : start + CHUNK, :] = (total[:, :HD] / total[:, HD:]).astype(jnp.bfloat16)

        scores = scores_of(0)
        for start in range(0, block_len, CHUNK):
            later = scores_of(start + CHUNK) if start + CHUNK < block_len else None
            finish(start, scores)
            scores = later
        return 0

    lax.fori_loop(0, members, unit, 0, unroll=4)


def square_kernel(attended, out):
    ones = jnp.ones((8, HD), jnp.bfloat16)
    total = None
    for h in range(attended.shape[0]):
        wide = attended[h, 0].astype(jnp.float32)
        square = wide * wide
        high = square.astype(jnp.bfloat16)
        low = (square - high.astype(jnp.float32)).astype(jnp.bfloat16)
        for part in (high, low):
            term = lax.dot_general(ones, part, (((1,), (1,)), ((), ())), preferred_element_type=jnp.float32)
            total = term if total is None else total + term
    out[...] = total


def norm_kernel(near, far, attended, gain, out, *, features):
    power = (near[...] + far[...]) / features
    factor = jnp.transpose(lax.rsqrt(power + EPS))[:, :1]
    for h in range(attended.shape[0]):
        columns = slice(h * HD, (h + 1) * HD)
        scaled = attended[h, 0].astype(jnp.float32) * factor * gain[:, columns].astype(jnp.float32)
        out[:, columns] = scaled.astype(jnp.bfloat16)


def call(kernel, shape, dtype, *args, scalars=(), scratch=()):
    vmem = pl.BlockSpec(memory_space=pltpu.VMEM)
    smem = pl.BlockSpec(memory_space=pltpu.SMEM)
    return pl.pallas_call(
        kernel,
        out_shape=jax.ShapeDtypeStruct(shape, dtype),
        in_specs=[smem] * len(scalars) + [vmem] * len(args),
        out_specs=vmem,
        scratch_shapes=list(scratch),
        compiler_params=pltpu.CompilerParams(vmem_limit_bytes=VMEM_LIMIT),
    )(*scalars, *args)


def local(query_keys, values, norm_gain, plan):
    size = lax.axis_size("seq")
    head_size = lax.axis_size("head")
    block_len, local_width = query_keys.shape
    heads = local_width // HD

    chip_bits = size.bit_length() - 2
    planes = planes_of(chip_bits)
    swaps = [swap_all(groups_of(size, 2 * u, 2 * v)) for u, v, _, _ in planes]
    smem = pl.BlockSpec(memory_space=pltpu.SMEM)
    table = jnp.asarray(lookup(chip_bits, planes))
    vmem = pl.BlockSpec(memory_space=pltpu.VMEM)
    hbm = pl.BlockSpec(memory_space=pltpu.HBM)
    packed, plane, ids = pl.pallas_call(
        pack_kernel,
        out_shape=(
            jax.ShapeDtypeStruct((heads, 2, block_len, HD), jnp.bfloat16),
            jax.ShapeDtypeStruct((1,), jnp.int32),
            jax.ShapeDtypeStruct((2,), jnp.int32),
        ),
        in_specs=[hbm] * 4,
        out_specs=(vmem, smem, smem),
        scratch_shapes=[
            pltpu.SMEM(plan.shape, jnp.int32),
            pltpu.SMEM(table.shape, jnp.int32),
            pltpu.SemaphoreType.DMA((2, heads)),
            pltpu.SemaphoreType.DMA((2,)),
        ],
        cost_estimate=pl.CostEstimate(flops=0, bytes_accessed=0, transcendentals=0),
        compiler_params=pltpu.CompilerParams(vmem_limit_bytes=PACK_VMEM_LIMIT),
    )(plan, table, query_keys, values)
    plane = plane.reshape(())
    routes = [head_swaps, *swaps]

    def exchange(step, sent):
        return call(
            step_kernel,
            packed.shape,
            jnp.bfloat16,
            lax.switch(plane, routes, sent),
            scalars=(step.reshape(1), ids),
            scratch=(pltpu.VMEM((heads, block_len, HD + LANES), jnp.bfloat16),),
        )

    mine = lax.fori_loop(0, 2, exchange, packed)
    squares = call(square_kernel, (8, block_len), jnp.float32, mine)
    near = squares + over_head(squares, 1)
    far = over_head(near, 3)
    return call(
        functools.partial(norm_kernel, features=local_width * head_size),
        (block_len, local_width),
        jnp.bfloat16,
        near,
        far,
        mine,
        norm_gain.reshape(1, local_width),
    )


def solution(mesh):
    in_specs = (P("seq", "head"), P("seq", "head"), P("head"), P())
    return jax.shard_map(local, mesh=mesh, in_specs=in_specs, out_specs=P("seq", "head"), check_vma=False)
```

```python
import functools

import jax
import jax.numpy as jnp
import numpy as np
from jax import lax
from jax.experimental import pallas as pl
from jax.experimental.pallas import tpu as pltpu
from jax.sharding import PartitionSpec as P

HD = 128
LANES = 128
EPS = 1e-6
SCALE = HD**-0.5 * float(np.log2(np.e))
VMEM_LIMIT = 40 * 1024 * 1024
PACK_VMEM_LIMIT = 61 * 1024 * 1024
CHUNK = 256


def planes_of(bits):
    found = []
    for v in range(1, 1 << bits):
        q = v.bit_length() - 1
        for u in range(1, 1 << bits):
            p = u.bit_length() - 1
            if p > q and not (u >> q) & 1:
                found.append((u, v, p, q))
    return found


def lookup(bits, planes):
    size = 1 << bits
    entry = {}
    for number, (u, v, p, q) in enumerate(planes):
        for a in (u, v, u ^ v):
            for b in (u, v, u ^ v):
                if a != b:
                    entry[a, b] = (number + 1) << 6 | (p + 1) << 3 | q + 1
    table = np.zeros((size, size), np.int32)
    for first in range(size):
        for second in range(size):
            a, b = first, second
            if a | b:
                if (a, b) not in entry:
                    a |= b
                    b = 1 if a != 1 else 2
                table[first, second] = entry[a, b]
    return table


def groups_of(size, u, v):
    span = [c ^ s ^ t for t in (0, v) for s in (0, u) for c in (0, 1)]
    seen, groups = set(), []
    for block in range(size):
        if block not in seen:
            base = block
            for mask in (u, v, 1):
                base = min(base, base ^ mask)
            coset = [base ^ mask for mask in span]
            seen |= set(coset)
            groups.append(coset)
    return groups


def swap_all(groups):
    def run(parts):
        return lax.all_to_all(parts, "seq", 0, 0, axis_index_groups=groups, tiled=True)

    return run


def over_head(values, bit_mask):
    return lax.ppermute(values, "head", [(i, i ^ bit_mask) for i in range(lax.axis_size("head"))])


def head_swaps(parts):
    return over_head(over_head(parts, 1), 3)


def pack_kernel(plan_in, table_in, query_keys, values, out, plane, ids, plan, table, held, sems, scalar_sems):
    scalars = [
        pltpu.make_async_copy(plan_in, plan, scalar_sems.at[0]),
        pltpu.make_async_copy(table_in, table, scalar_sems.at[1]),
    ]
    for copy in scalars:
        copy.start()
    copies = []
    chunks = sems.shape[1]
    size = out.shape[2] // chunks
    for chunk in range(chunks):
        rows = slice(chunk * size, (chunk + 1) * size)
        for part, array in enumerate((query_keys, values)):
            copy = pltpu.make_async_copy(array.at[rows], held.at[part, rows], sems.at[part, chunk])
            copy.start()
            copies.append((copy, part, rows))
    for copy in scalars:
        copy.wait()
    first, second = plan[0, 0], plan[1, 0]
    entry = table[first >> 1, second >> 1]
    p, q = (entry >> 3) & 7, entry & 7
    plane[0] = entry >> 6
    for i, mask in enumerate((first, second)):
        ids[i] = (mask & 1) | (((mask >> p) & 1) << 1) | (((mask >> q) & 1) << 2)
    for copy, part, rows in copies:
        copy.wait()
        for h in range(out.shape[0]):
            out[h, part, rows] = held[part, rows, h * HD : (h + 1) * HD]


def step_kernel(step, ids, arrived, out, ext):
    pl.when(step[0] == 0)(lambda: attend(ids, arrived, out, ext))

    @pl.when(step[0] != 0)
    def _():
        for h in range(arrived.shape[0]):
            out[h, 0] = arrived[h, 0]


def attend(ids, blocks, out, ext):
    members, _, block_len, _ = blocks.shape
    for t in range(members):
        ext[t, :, :HD] = blocks[t, 1]
        ext[t, :, HD:] = jnp.ones((block_len, LANES), jnp.bfloat16)
    row_ids = lax.broadcasted_iota(jnp.int32, (CHUNK, CHUNK), 0)
    col_ids = lax.broadcasted_iota(jnp.int32, (CHUNK, CHUNK), 1)
    diagonal = row_ids == col_ids

    def unit(t, _):
        others = (t, t ^ ids[0], t ^ ids[1])

        def scores_of(start):
            rows = blocks[t, 0, start : start + CHUNK, :]
            scores = [
                lax.dot_general(
                    rows, blocks[other, 0], (((1,), (1,)), ((), ())), preferred_element_type=jnp.float32
                )
                for other in others
            ]
            pieces = [scores[0][:, c : c + CHUNK] for c in range(0, block_len, CHUNK)]
            pieces[start // CHUNK] = jnp.where(diagonal, -jnp.inf, pieces[start // CHUNK])
            scores[0] = jnp.concatenate(pieces, axis=1)
            return scores

        def finish(start, scores):
            peak = functools.reduce(jnp.maximum, scores)
            peak = jnp.max(peak, axis=1, keepdims=True) * SCALE
            total = None
            for score, other in zip(scores, others, strict=True):
                weight = jnp.exp2(score * SCALE - peak).astype(jnp.bfloat16)
                part = jnp.dot(weight, ext[other], preferred_element_type=jnp.float32)
                total = part if total is None else total + part
            out[t, 0, start : start + CHUNK, :] = (total[:, :HD] / total[:, HD:]).astype(jnp.bfloat16)

        scores = scores_of(0)
        for start in range(0, block_len, CHUNK):
            later = scores_of(start + CHUNK) if start + CHUNK < block_len else None
            finish(start, scores)
            scores = later
        return 0

    lax.fori_loop(0, members, unit, 0, unroll=4)


def square_kernel(attended, out):
    ones = jnp.ones((8, HD), jnp.bfloat16)
    total = None
    for h in range(attended.shape[0]):
        wide = attended[h, 0].astype(jnp.float32)
        square = wide * wide
        high = square.astype(jnp.bfloat16)
        low = (square - high.astype(jnp.float32)).astype(jnp.bfloat16)
        for part in (high, low):
            term = lax.dot_general(ones, part, (((1,), (1,)), ((), ())), preferred_element_type=jnp.float32)
            total = term if total is None else total + term
    out[...] = total[:1]


def norm_kernel(near, far, attended, gain, out, held, sems, *, features):
    power = (near[...] + far[...]) / features
    factor = lax.rsqrt(power + EPS)
    factor = jnp.transpose(jnp.broadcast_to(factor, (8, factor.shape[1])))[:, :1]
    copies = []
    for part in range(sems.shape[0]):
        size = out.shape[0] // sems.shape[0]
        rows = slice(part * size, (part + 1) * size)
        for h in range(attended.shape[0]):
            columns = slice(h * HD, (h + 1) * HD)
            scaled = attended[h, 0, rows].astype(jnp.float32) * factor[rows] * gain[:, columns].astype(jnp.float32)
            held[rows, columns] = scaled.astype(jnp.bfloat16)
        copies.append(pltpu.make_async_copy(held.at[rows], out.at[rows], sems.at[part]))
        copies[-1].start()
    for copy in copies:
        copy.wait()


def call(kernel, shape, dtype, *args, scalars=(), scratch=()):
    vmem = pl.BlockSpec(memory_space=pltpu.VMEM)
    smem = pl.BlockSpec(memory_space=pltpu.SMEM)
    return pl.pallas_call(
        kernel,
        out_shape=jax.ShapeDtypeStruct(shape, dtype),
        in_specs=[smem] * len(scalars) + [vmem] * len(args),
        out_specs=vmem,
        scratch_shapes=list(scratch),
        compiler_params=pltpu.CompilerParams(vmem_limit_bytes=VMEM_LIMIT),
    )(*scalars, *args)


def local(query_keys, values, norm_gain, plan):
    size = lax.axis_size("seq")
    head_size = lax.axis_size("head")
    block_len, local_width = query_keys.shape
    heads = local_width // HD

    chip_bits = size.bit_length() - 2
    planes = planes_of(chip_bits)
    swaps = [swap_all(groups_of(size, 2 * u, 2 * v)) for u, v, _, _ in planes]
    smem = pl.BlockSpec(memory_space=pltpu.SMEM)
    table = jnp.asarray(lookup(chip_bits, planes))
    vmem = pl.BlockSpec(memory_space=pltpu.VMEM)
    hbm = pl.BlockSpec(memory_space=pltpu.HBM)
    packed, plane, ids = pl.pallas_call(
        pack_kernel,
        out_shape=(
            jax.ShapeDtypeStruct((heads, 2, block_len, HD), jnp.bfloat16),
            jax.ShapeDtypeStruct((1,), jnp.int32),
            jax.ShapeDtypeStruct((2,), jnp.int32),
        ),
        in_specs=[hbm] * 4,
        out_specs=(vmem, smem, smem),
        scratch_shapes=[
            pltpu.SMEM(plan.shape, jnp.int32),
            pltpu.SMEM(table.shape, jnp.int32),
            pltpu.VMEM((2, block_len, local_width), jnp.bfloat16),
            pltpu.SemaphoreType.DMA((2, 8)),
            pltpu.SemaphoreType.DMA((2,)),
        ],
        cost_estimate=pl.CostEstimate(flops=0, bytes_accessed=0, transcendentals=0),
        compiler_params=pltpu.CompilerParams(vmem_limit_bytes=PACK_VMEM_LIMIT),
    )(plan, table, query_keys, values)
    plane = plane.reshape(())
    routes = [head_swaps, *swaps]

    def exchange(step, sent):
        return call(
            step_kernel,
            packed.shape,
            jnp.bfloat16,
            lax.switch(plane, routes, sent),
            scalars=(step.reshape(1), ids),
            scratch=(pltpu.VMEM((heads, block_len, HD + LANES), jnp.bfloat16),),
        )

    mine = lax.fori_loop(0, 2, exchange, packed)
    squares = call(square_kernel, (1, block_len), jnp.float32, mine)
    near = squares + over_head(squares, 1)
    far = over_head(near, 3)
    return pl.pallas_call(
        functools.partial(norm_kernel, features=local_width * head_size),
        out_shape=jax.ShapeDtypeStruct((block_len, local_width), jnp.bfloat16),
        in_specs=[vmem] * 4,
        out_specs=hbm,
        scratch_shapes=[
            pltpu.VMEM((block_len, local_width), jnp.bfloat16),
            pltpu.SemaphoreType.DMA((8,)),
        ],
        compiler_params=pltpu.CompilerParams(vmem_limit_bytes=VMEM_LIMIT),
    )(near, far, mine, norm_gain.reshape(1, local_width))


def solution(mesh):
    in_specs = (P("seq", "head"), P("seq", "head"), P("head"), P())
    return jax.shard_map(local, mesh=mesh, in_specs=in_specs, out_specs=P("seq", "head"), check_vma=False)
```

```python
import functools

import jax
import jax.numpy as jnp
import numpy as np
from jax import lax
from jax.experimental import pallas as pl
from jax.experimental.pallas import tpu as pltpu
from jax.sharding import PartitionSpec as P

HD = 128
LANES = 128
EPS = 1e-6
SCALE = HD**-0.5 * float(np.log2(np.e))
VMEM_LIMIT = 40 * 1024 * 1024
PACK_VMEM_LIMIT = 61 * 1024 * 1024
CHUNK = 256


def planes_of(bits):
    found = []
    for v in range(1, 1 << bits):
        q = v.bit_length() - 1
        for u in range(1, 1 << bits):
            p = u.bit_length() - 1
            if p > q and not (u >> q) & 1:
                found.append((u, v, p, q))
    return found


def lookup(bits, planes):
    size = 1 << bits
    entry = {}
    for number, (u, v, p, q) in enumerate(planes):
        for a in (u, v, u ^ v):
            for b in (u, v, u ^ v):
                if a != b:
                    entry[a, b] = (number + 1) << 6 | (p + 1) << 3 | q + 1
    table = np.zeros((size, size), np.int32)
    for first in range(size):
        for second in range(size):
            a, b = first, second
            if a | b:
                if (a, b) not in entry:
                    a |= b
                    b = 1 if a != 1 else 2
                table[first, second] = entry[a, b]
    return table


def groups_of(size, u, v):
    span = [c ^ s ^ t for t in (0, v) for s in (0, u) for c in (0, 1)]
    seen, groups = set(), []
    for block in range(size):
        if block not in seen:
            base = block
            for mask in (u, v, 1):
                base = min(base, base ^ mask)
            coset = [base ^ mask for mask in span]
            seen |= set(coset)
            groups.append(coset)
    return groups


def swap_all(groups):
    def run(parts):
        return lax.all_to_all(parts, "seq", 0, 0, axis_index_groups=groups, tiled=True)

    return run


def over_head(values, bit_mask):
    return lax.ppermute(values, "head", [(i, i ^ bit_mask) for i in range(lax.axis_size("head"))])


def head_swaps(parts):
    return over_head(over_head(parts, 1), 3)


def pack_kernel(plan_in, table_in, query_keys, values, out, plane_out, ids_out, plan, table, plane, ids, held, sems, scalar_sems):
    scalars = [
        pltpu.make_async_copy(plan_in, plan, scalar_sems.at[0]),
        pltpu.make_async_copy(table_in, table, scalar_sems.at[1]),
    ]
    for copy in scalars:
        copy.start()
    copies = []
    chunks = sems.shape[1]
    size = out.shape[2] // chunks
    for chunk in range(chunks):
        rows = slice(chunk * size, (chunk + 1) * size)
        for part, array in enumerate((query_keys, values)):
            copy = pltpu.make_async_copy(array.at[rows], held.at[part, rows], sems.at[part, chunk])
            copy.start()
            copies.append((copy, part, rows))
    for copy in scalars:
        copy.wait()
    first, second = plan[0, 0], plan[1, 0]
    entry = table[first >> 1, second >> 1]
    p, q = (entry >> 3) & 7, entry & 7
    plane[0] = entry >> 6
    for i, mask in enumerate((first, second)):
        ids[i] = (mask & 1) | (((mask >> p) & 1) << 1) | (((mask >> q) & 1) << 2)
    results = [
        pltpu.make_async_copy(plane, plane_out, scalar_sems.at[2]),
        pltpu.make_async_copy(ids, ids_out, scalar_sems.at[3]),
    ]
    for copy in results:
        copy.start()
    for copy, part, rows in copies:
        copy.wait()
        for h in range(out.shape[0]):
            out[h, part, rows] = held[part, rows, h * HD : (h + 1) * HD]
    for copy in results:
        copy.wait()


def step_kernel(step, ids, arrived, out, ext):
    pl.when(step[0] == 0)(lambda: attend(ids, arrived, out, ext))

    @pl.when(step[0] != 0)
    def _():
        for h in range(arrived.shape[0]):
            out[h, 0] = arrived[h, 0]


def attend(ids, blocks, out, ext):
    members, _, block_len, _ = blocks.shape
    for t in range(members):
        ext[t, :, :HD] = blocks[t, 1]
        ext[t, :, HD:] = jnp.ones((block_len, LANES), jnp.bfloat16)
    row_ids = lax.broadcasted_iota(jnp.int32, (CHUNK, CHUNK), 0)
    col_ids = lax.broadcasted_iota(jnp.int32, (CHUNK, CHUNK), 1)
    diagonal = row_ids == col_ids

    def unit(t, _):
        others = (t, t ^ ids[0], t ^ ids[1])

        def scores_of(start):
            rows = blocks[t, 0, start : start + CHUNK, :]
            scores = [
                lax.dot_general(
                    rows, blocks[other, 0], (((1,), (1,)), ((), ())), preferred_element_type=jnp.float32
                )
                for other in others
            ]
            pieces = [scores[0][:, c : c + CHUNK] for c in range(0, block_len, CHUNK)]
            pieces[start // CHUNK] = jnp.where(diagonal, -jnp.inf, pieces[start // CHUNK])
            scores[0] = jnp.concatenate(pieces, axis=1)
            return scores

        def finish(start, scores):
            peak = functools.reduce(jnp.maximum, scores)
            peak = jnp.max(peak, axis=1, keepdims=True) * SCALE
            total = None
            for score, other in zip(scores, others, strict=True):
                weight = jnp.exp2(score * SCALE - peak).astype(jnp.bfloat16)
                part = jnp.dot(weight, ext[other], preferred_element_type=jnp.float32)
                total = part if total is None else total + part
            out[t, 0, start : start + CHUNK, :] = (total[:, :HD] / total[:, HD:]).astype(jnp.bfloat16)

        scores = scores_of(0)
        for start in range(0, block_len, CHUNK):
            later = scores_of(start + CHUNK) if start + CHUNK < block_len else None
            finish(start, scores)
            scores = later
        return 0

    lax.fori_loop(0, members, unit, 0, unroll=4)


def square_kernel(attended, out):
    ones = jnp.ones((8, HD), jnp.bfloat16)
    total = None
    for h in range(attended.shape[0]):
        wide = attended[h, 0].astype(jnp.float32)
        square = wide * wide
        high = square.astype(jnp.bfloat16)
        low = (square - high.astype(jnp.float32)).astype(jnp.bfloat16)
        for part in (high, low):
            term = lax.dot_general(ones, part, (((1,), (1,)), ((), ())), preferred_element_type=jnp.float32)
            total = term if total is None else total + term
    out[...] = total[:1]


def norm_kernel(near, far, attended, gain, out, held, sems, *, features):
    power = (near[...] + far[...]) / features
    factor = lax.rsqrt(power + EPS)
    factor = jnp.transpose(jnp.broadcast_to(factor, (8, factor.shape[1])))[:, :1]
    copies = []
    for part in range(sems.shape[0]):
        size = out.shape[0] // sems.shape[0]
        rows = slice(part * size, (part + 1) * size)
        for h in range(attended.shape[0]):
            columns = slice(h * HD, (h + 1) * HD)
            scaled = attended[h, 0, rows].astype(jnp.float32) * factor[rows] * gain[:, columns].astype(jnp.float32)
            held[rows, columns] = scaled.astype(jnp.bfloat16)
        copies.append(pltpu.make_async_copy(held.at[rows], out.at[rows], sems.at[part]))
        copies[-1].start()
    for copy in copies:
        copy.wait()


def call(kernel, shape, dtype, *args, scalars=(), scratch=()):
    vmem = pl.BlockSpec(memory_space=pltpu.VMEM)
    smem = pl.BlockSpec(memory_space=pltpu.SMEM)
    return pl.pallas_call(
        kernel,
        out_shape=jax.ShapeDtypeStruct(shape, dtype),
        in_specs=[smem] * len(scalars) + [vmem] * len(args),
        out_specs=vmem,
        scratch_shapes=list(scratch),
        compiler_params=pltpu.CompilerParams(vmem_limit_bytes=VMEM_LIMIT),
    )(*scalars, *args)


def local(query_keys, values, norm_gain, plan):
    size = lax.axis_size("seq")
    head_size = lax.axis_size("head")
    block_len, local_width = query_keys.shape
    heads = local_width // HD

    chip_bits = size.bit_length() - 2
    planes = planes_of(chip_bits)
    swaps = [swap_all(groups_of(size, 2 * u, 2 * v)) for u, v, _, _ in planes]
    smem = pl.BlockSpec(memory_space=pltpu.SMEM)
    table = jnp.asarray(lookup(chip_bits, planes))
    vmem = pl.BlockSpec(memory_space=pltpu.VMEM)
    hbm = pl.BlockSpec(memory_space=pltpu.HBM)
    packed, plane, ids = pl.pallas_call(
        pack_kernel,
        out_shape=(
            jax.ShapeDtypeStruct((heads, 2, block_len, HD), jnp.bfloat16),
            jax.ShapeDtypeStruct((1,), jnp.int32),
            jax.ShapeDtypeStruct((2,), jnp.int32),
        ),
        in_specs=[hbm] * 4,
        out_specs=(vmem, hbm, hbm),
        scratch_shapes=[
            pltpu.SMEM(plan.shape, jnp.int32),
            pltpu.SMEM(table.shape, jnp.int32),
            pltpu.SMEM((1,), jnp.int32),
            pltpu.SMEM((2,), jnp.int32),
            pltpu.VMEM((2, block_len, local_width), jnp.bfloat16),
            pltpu.SemaphoreType.DMA((2, 8)),
            pltpu.SemaphoreType.DMA((4,)),
        ],
        cost_estimate=pl.CostEstimate(flops=0, bytes_accessed=0, transcendentals=0),
        compiler_params=pltpu.CompilerParams(vmem_limit_bytes=PACK_VMEM_LIMIT),
    )(plan, table, query_keys, values)
    plane = plane.reshape(())
    routes = [head_swaps, *swaps]

    def exchange(step, sent):
        return call(
            step_kernel,
            packed.shape,
            jnp.bfloat16,
            lax.switch(plane, routes, sent),
            scalars=(step.reshape(1), ids),
            scratch=(pltpu.VMEM((heads, block_len, HD + LANES), jnp.bfloat16),),
        )

    mine = lax.fori_loop(0, 2, exchange, packed)
    squares = call(square_kernel, (1, block_len), jnp.float32, mine)
    near = squares + over_head(squares, 1)
    far = over_head(near, 3)
    return pl.pallas_call(
        functools.partial(norm_kernel, features=local_width * head_size),
        out_shape=jax.ShapeDtypeStruct((block_len, local_width), jnp.bfloat16),
        in_specs=[vmem] * 4,
        out_specs=hbm,
        scratch_shapes=[
            pltpu.VMEM((block_len, local_width), jnp.bfloat16),
            pltpu.SemaphoreType.DMA((8,)),
        ],
        compiler_params=pltpu.CompilerParams(vmem_limit_bytes=VMEM_LIMIT),
    )(near, far, mine, norm_gain.reshape(1, local_width))


def solution(mesh):
    in_specs = (P("seq", "head"), P("seq", "head"), P("head"), P())
    return jax.shard_map(local, mesh=mesh, in_specs=in_specs, out_specs=P("seq", "head"), check_vma=False)
```
